32 devices in a mesh: band: 4 (over x, core), feed: 8 (over z, y).
Axes of the slice: x: 2, y: 2, z: 4, core: 2. Of those that a mesh axis runs over, the one named last changes fastest.
Arguments:
- voltages: float32 [768, 2048, 128], P('band', 'feed'), may hold values from -6 to 6
- feed_cells: int32 [4096], replicated, may hold values from 0 to 4095, each once
- delays: int32 [768, 256], P('band'), may hold values from 0 to 63
Outputs:
- dedispersed: float32 [256, 1024, 64], P('band', 'feed')
The draws below stay inside these ranges and needn't reach their ends.
Inputs may be any that keep to these rules, and one draw needn't show every extreme that they name: `feed_cells`: a permutation of the cells of the 64 x 64 feed grid, so no two feeds share a cell.
All inputs are finite; a program needn't handle non-finite values.
Results may differ from the reference program's by a relative error of at most 0.0003.
Values sent between devices are 32-bit elements; how exact they have to be, the bound alone decides.
No kernel may reach another device: no remote copies, remote signals or barrier semaphores. Data moves between devices by JAX's collectives and lax.ppermute only.
A program may use at most 128 MiB of HBM per device.

```python
import math
import jax
import jax.numpy as jnp
from jax import lax

FEEDS = 2048
CHANNELS = 768
FRAMES = 64
SIDE = 32
BEAMS = 1024
TRIALS = 256
GRID = 64


def with_ends(result, rng, smallest, high):
    index_at = [jax.random.randint(jax.random.fold_in(rng, axis), (), 0, length) for axis, length in enumerate(result.shape)]
    widest = result.shape.index(max(result.shape))
    neighbour = index_at[:widest] + [(index_at[widest] + 1) % result.shape[widest]] + index_at[widest + 1:]
    return result.at[tuple(index_at)].set(smallest).at[tuple(neighbour)].set(high)


def steps_of(key, shape, split, least, largest):
    factor_of = 1.0
    for position, parts in split:
        steps = jax.random.uniform(jax.random.fold_in(jax.random.fold_in(key, 6), position), (parts,), jnp.float32, least / len(split), largest / len(split))
        factor_of = factor_of * jnp.repeat(jnp.exp(steps), shape[position] // parts).reshape((-1,) + (1,) * (len(shape) - 1 - position))
    return factor_of


def scatter_about(rng, shape, spread, limit, split=(), kind=jnp.bfloat16):
    factor_of = steps_of(rng, shape, split, -0.22, 0.18) if split else 1.0
    entries = jax.random.normal(rng, shape, jnp.float32) * spread * factor_of
    return jnp.minimum(jnp.maximum(entries, -limit), limit).astype(kind)


def setup_inputs(seed: int = 0) -> dict:
    key_list = jax.random.split(jax.random.key(seed), 4)
    voltages = scatter_about(key_list[0], (CHANNELS, FEEDS, 2 * FRAMES), 1.0, 6.0, ((0, 4), (1, 8)), jnp.float32)
    feed_cells = jax.random.permutation(key_list[1], GRID * GRID).astype(jnp.int32)
    delays = with_ends(jax.random.randint(key_list[2], (CHANNELS, TRIALS), 0, FRAMES), jax.random.fold_in(key_list[2], 1), 0, FRAMES - 1).astype(jnp.int32)
    return dict(voltages=voltages, feed_cells=feed_cells, delays=delays)


def feed_offsets(feed_cells):
    cell_index = feed_cells[:FEEDS]
    cell_row = cell_index // GRID
    cell_col = cell_index % GRID
    beam_ids = jnp.arange(BEAMS, dtype=jnp.int32)
    beam_row = beam_ids // SIDE - SIDE // 2
    beam_col = beam_ids % SIDE - SIDE // 2
    return beam_row[:, None] * cell_row[None, :] + beam_col[:, None] * cell_col[None, :]

def steering(offsets, channel):
    residue = jnp.mod(offsets * (CHANNELS + channel), GRID * CHANNELS)
    phases = residue.astype(jnp.float32) * (2.0 * math.pi / (GRID * CHANNELS))
    factor = 1.0 / math.sqrt(FEEDS)
    return (jnp.cos(phases) * factor, jnp.sin(phases) * factor)

def reference(voltages, feed_cells, delays):
    highest = lax.Precision.HIGHEST
    offsets = feed_offsets(feed_cells)

    def beam_power(item):
        channel, voltage = item
        cosine, sine_part = steering(offsets, channel)
        with_cos = jnp.dot(cosine, voltage, precision=highest)
        with_sin = jnp.dot(sine_part, voltage, precision=highest)
        real_part = with_cos[:, :FRAMES] + with_sin[:, FRAMES:]
        imag_part = with_cos[:, FRAMES:] - with_sin[:, :FRAMES]
        return real_part * real_part + imag_part * imag_part
    powers = lax.map(beam_power, (jnp.arange(CHANNELS, dtype=jnp.int32), voltages))
    centred = powers - lax.optimization_barrier(jnp.mean(powers, axis=2, keepdims=True))
    frame_ids = jnp.arange(FRAMES, dtype=jnp.int32)
    wave = jnp.mod(frame_ids[:, None] * frame_ids[None, :], FRAMES).astype(jnp.float32) * (2.0 * math.pi / FRAMES)
    forward = jnp.concatenate([jnp.cos(wave), -jnp.sin(wave)], axis=1)
    spectra = jnp.dot(centred.reshape(CHANNELS * BEAMS, FRAMES), forward, precision=highest)
    spectra = spectra.reshape(CHANNELS, BEAMS, 2 * FRAMES)

    def one_bin(bin_index):
        residue = jnp.mod(delays * bin_index, FRAMES)
        phases = residue.astype(jnp.float32) * (2.0 * math.pi / FRAMES)
        shift_cos = jnp.cos(phases).T
        shift_sin = jnp.sin(phases).T
        spec_real = lax.dynamic_index_in_dim(spectra, bin_index, 2, False)
        spec_imag = lax.dynamic_index_in_dim(spectra, bin_index + FRAMES, 2, False)
        out_real = jnp.dot(shift_cos, spec_real, precision=highest) - jnp.dot(shift_sin, spec_imag, precision=highest)
        out_imag = jnp.dot(shift_cos, spec_imag, precision=highest) + jnp.dot(shift_sin, spec_real, precision=highest)
        return (out_real, out_imag)
    bins_real, bins_imag = lax.map(one_bin, frame_ids)
    series = jnp.einsum('kdb,kt->dbt', bins_real, jnp.cos(wave), precision=highest)
    series = series - jnp.einsum('kdb,kt->dbt', bins_imag, jnp.sin(wave), precision=highest)
    return series * (0.5 / (FRAMES * math.sqrt(CHANNELS)))
```

```python
import functools
import math

import jax
import jax.numpy as jnp
from jax import lax
from jax.experimental import pallas as pl
from jax.experimental.pallas import tpu as pltpu
from jax.sharding import PartitionSpec as P

FEEDS = 2048
CHANNELS = 768
FRAMES = 64
SIDE = 32
BEAMS = 1024
GRID = 64
BINS = FRAMES // 2
LANES = 2 * FRAMES
CHUNK = 8
VMEM_LIMIT = 56 * 1024 * 1024


def high_low(table):
    high = lax.reduce_precision(table, 8, 7)
    return high.astype(jnp.bfloat16), (table - high).astype(jnp.bfloat16)


def halves(values):
    high = values.astype(jnp.bfloat16)
    return high, (values - high.astype(jnp.float32)).astype(jnp.bfloat16)


def steering_tables(channels, offsets):
    lines = jnp.arange(GRID, dtype=jnp.int32)
    residue = jnp.mod(
        offsets[None, :, None] * lines[None, None, :] * (CHANNELS + channels)[:, None, None],
        GRID * CHANNELS,
    )
    phases = residue.astype(jnp.float32) * (2.0 * math.pi / (GRID * CHANNELS))
    high, low = high_low(jnp.concatenate([jnp.cos(phases), jnp.sin(phases)], axis=1))
    return jnp.concatenate([high, high, low], axis=2)


def turned(values):
    swapped = pltpu.roll(values, FRAMES, 1)
    lane = lax.broadcasted_iota(jnp.int32, swapped.shape, 1)
    return jnp.where(lane < FRAMES, swapped, -swapped)


def partial_kernel(cells_ref, *refs, senders, wide):
    volts_ref, first_ref, second_ref = refs[:3]
    mine_ref, theirs_ref, grid_ref, rows_ref = refs[-4:]
    _, kc, feeds_each, _ = volts_ref.shape
    cells = GRID * GRID

    @pl.when(pl.program_id(0) == 0)
    def _():
        grid_ref[...] = jnp.zeros_like(grid_ref)

    for sender in range(senders):

        volts = volts_ref.at[sender].reshape(kc * feeds_each, LANES)

        def place(feed, _, sender=sender, volts=volts):
            cell = cells_ref[sender * feeds_each + feed]
            value = volts[pl.ds(feed, kc, stride=feeds_each), :]
            grid_ref[pl.ds(cell, kc, stride=cells), :] = value
            return 0

        lax.fori_loop(0, feeds_each, place, 0, unroll=8)

    def one_channel(chan, _):
        first = first_ref[chan]
        second = second_ref[chan]

        def column_step(step, _):
            base = chan * cells + step * (wide * GRID)
            block = jnp.concatenate(
                [grid_ref[pl.ds(base + j * GRID, GRID), :] for j in range(wide)], axis=1
            )
            high, low = halves(block)
            sums = jnp.dot(
                first, jnp.concatenate([high, low, high], axis=0), preferred_element_type=jnp.float32
            )
            for j in range(wide):
                part = sums[:, j * LANES : (j + 1) * LANES]
                rows_ref[pl.ds(step * wide + j, SIDE, stride=GRID), :] = part[:SIDE] + turned(part[SIDE:])
            return 0

        lax.fori_loop(0, GRID // wide, column_step, 0, unroll=True)

        def row_step(step, _):
            base = step * (wide * GRID)
            block = jnp.concatenate(
                [rows_ref[pl.ds(base + j * GRID, GRID), :] for j in range(wide)], axis=1
            )
            high, low = halves(block)
            sums = jnp.dot(
                second, jnp.concatenate([high, low, high], axis=0), preferred_element_type=jnp.float32
            )
            for j in range(wide):
                part = sums[:, j * LANES : (j + 1) * LANES]
                beams = part[:SIDE] + turned(part[SIDE:])
                at = chan * (SIDE // 2 * SIDE) + step * wide + j
                mine_ref[pl.ds(at, SIDE // 2, stride=SIDE), :] = beams[: SIDE // 2]
                theirs_ref[pl.ds(at, SIDE // 2, stride=SIDE), :] = beams[SIDE // 2 :]
            return 0

        lax.fori_loop(0, SIDE // wide, row_step, 0, unroll=True)
        return 0

    lax.fori_loop(0, kc, one_channel, 0)


def partial_beams(cells, volts, first, second, kc, after, wide=4):
    senders, cc, feeds_each, _ = volts.shape
    rows = SIDE // 2 * SIDE
    out = jax.ShapeDtypeStruct((cc * rows, LANES), jnp.float32)
    table_spec = pl.BlockSpec((kc,) + first.shape[1:], lambda i, *_: (i, 0, 0))
    out_spec = pl.BlockSpec((kc * rows, LANES), lambda i, *_: (i, 0))
    return pl.pallas_call(
        functools.partial(partial_kernel, senders=senders, wide=wide),
        grid_spec=pltpu.PrefetchScalarGridSpec(
            num_scalar_prefetch=1,
            grid=(cc // kc,),
            in_specs=[
                pl.BlockSpec((senders, kc, feeds_each, LANES), lambda i, *_: (0, i, 0, 0)),
                table_spec,
                table_spec,
            ]
            + [pl.BlockSpec(memory_space=pl.ANY)] * len(after),
            out_specs=[out_spec, out_spec],
            scratch_shapes=[
                pltpu.VMEM((kc * GRID * GRID, LANES), jnp.float32),
                pltpu.VMEM((SIDE * GRID, LANES), jnp.float32),
            ],
        ),
        out_shape=[out, out],
        compiler_params=pltpu.CompilerParams(vmem_limit_bytes=VMEM_LIMIT),
        cost_estimate=pl.CostEstimate(
            flops=cc * 6 * 50_000_000, bytes_accessed=volts.size * 4 + 2 * cc * rows * LANES * 4, transcendentals=0
        ),
        name="partial_beams",
    )(cells, volts, first, second, *after)


def forward_table():
    frames = jnp.arange(FRAMES, dtype=jnp.int32)
    wave = jnp.mod(frames[:, None] * (1 + jnp.arange(BINS, dtype=jnp.int32))[None, :], FRAMES)
    phases = wave.astype(jnp.float32) * (2.0 * math.pi / FRAMES)
    one = jnp.concatenate([jnp.cos(phases), -jnp.sin(phases)], axis=1)
    none = jnp.zeros_like(one)
    both = jnp.concatenate(
        [jnp.concatenate([one, none], axis=1), jnp.concatenate([none, one], axis=1)], axis=0
    )
    high, low = high_low(both)
    return jnp.concatenate([high, high, low], axis=0)


def inverse_table():
    frames = jnp.arange(FRAMES, dtype=jnp.int32)
    bins = 1 + jnp.arange(BINS, dtype=jnp.int32)
    wave = jnp.mod(frames[:, None] * bins[None, :], FRAMES)
    phases = wave.astype(jnp.float32) * (2.0 * math.pi / FRAMES)
    weight = jnp.where(bins < BINS, 2.0, 1.0) * (0.5 / (FRAMES * math.sqrt(CHANNELS) * FEEDS))
    high, low = high_low(jnp.concatenate([jnp.cos(phases) * weight, -jnp.sin(phases) * weight], axis=1))
    return jnp.concatenate([high, high, low], axis=1)


def spectra_kernel(mine_ref, came_ref, table_ref, *refs, kc, split_rows, owners):
    out_refs = refs[-owners:]
    each = out_refs[0].shape[1]
    rows = SIDE // 2 * SIDE
    for chan in range(kc):
        at = pl.ds(chan * rows, rows)
        beams = mine_ref[at, :] + came_ref[at, :]
        square = beams * beams
        power = square + pltpu.roll(square, FRAMES, 1)
        if split_rows:
            left, right = power[: rows // 2], power[rows // 2 :]
        else:
            power = power.reshape(SIDE // 2, 2, SIDE // 2, LANES)
            left = power[:, 0].reshape(rows // 2, LANES)
            right = power[:, 1].reshape(rows // 2, LANES)
        lane = lax.broadcasted_iota(jnp.int32, left.shape, 1)
        high, low = halves(jnp.where(lane < FRAMES, left, right))
        spectra = jnp.dot(
            jnp.concatenate([high, low, high], axis=1), table_ref[...], preferred_element_type=jnp.float32
        )
        for owner in range(owners):
            out_refs[owner][chan] = spectra[owner * each : (owner + 1) * each]


def beam_spectra(mine, came, table, owners, split_rows, kc, after):
    rows = SIDE // 2 * SIDE
    cc = mine.shape[0] // rows
    each = rows // 2 // owners
    block = pl.BlockSpec((kc * rows, LANES), lambda i: (i, 0))
    return pl.pallas_call(
        functools.partial(spectra_kernel, kc=kc, split_rows=split_rows, owners=owners),
        grid=(cc // kc,),
        in_specs=[block, block, pl.BlockSpec(table.shape, lambda i: (0, 0))]
        + [pl.BlockSpec(memory_space=pl.ANY)] * len(after),
        out_specs=[pl.BlockSpec((kc, each, LANES), lambda i: (i, 0, 0))] * owners,
        out_shape=[jax.ShapeDtypeStruct((cc, each, LANES), jnp.float32)] * owners,
        compiler_params=pltpu.CompilerParams(vmem_limit_bytes=VMEM_LIMIT),
        cost_estimate=pl.CostEstimate(
            flops=cc * rows * LANES * LANES * 3, bytes_accessed=mine.size * 12, transcendentals=0
        ),
        name="beam_spectra",
    )(mine, came, table, *after)


def dedisperse_kernel(*refs, chans, each, trials, first, last):
    spectra_ref, cos_ref, sin_ref, inverse_ref = refs[:4]
    held_ref = None if first else refs[4]
    out_ref, bins_ref = refs[-3 if last else -2], refs[-1 if not last else -2]
    total_ref = refs[-1] if last else out_ref
    stack = LANES // each

    def turn_step(step, _):
        block = jnp.transpose(spectra_ref[pl.ds(step * LANES, LANES), :])
        top, bottom = block[:FRAMES], block[FRAMES:]
        lane = lax.broadcasted_iota(jnp.int32, top.shape, 1)
        for e in range(stack):
            left = pltpu.roll(top, (LANES - e * each) % LANES, 1) if e else top
            shift = (each - e * each) % LANES
            right = pltpu.roll(bottom, shift, 1) if shift else bottom
            bins_ref[pl.ds(step * stack + e, FRAMES, stride=chans), :] = jnp.where(lane < each, left, right)
        return 0

    lax.fori_loop(0, chans // stack, turn_step, 0, unroll=4)

    cos_one, sin_one = cos_ref[...], sin_ref[...]

    def bin_step(k, carry):
        cos_k, sin_k = carry
        shift_high, shift_low = halves(jnp.concatenate([cos_k, sin_k], axis=0))
        spec = jnp.concatenate(
            [bins_ref[pl.ds(k * chans, chans), :], bins_ref[pl.ds((BINS + k) * chans, chans), :]], axis=1
        )
        high, low = halves(spec)
        if chans % LANES == 0:
            sums = jnp.dot(
                jnp.concatenate([shift_high, shift_high, shift_low], axis=1),
                jnp.concatenate([high, low, high], axis=0),
                preferred_element_type=jnp.float32,
            )
        else:
            sums = jnp.dot(shift_high, high, preferred_element_type=jnp.float32)
            sums = sums + jnp.dot(shift_high, low, preferred_element_type=jnp.float32)
            sums = sums + jnp.dot(shift_low, high, preferred_element_type=jnp.float32)
        real = sums[:trials, :LANES] - sums[trials:, LANES:]
        imag = sums[:trials, LANES:] + sums[trials:, :LANES]
        at_real, at_imag = pl.ds(k * trials, trials), pl.ds((BINS + k) * trials, trials)
        if held_ref is not None:
            real = real + held_ref[at_real, :]
            imag = imag + held_ref[at_imag, :]
        total_ref[at_real, :] = real
        total_ref[at_imag, :] = imag
        return cos_k * cos_one - sin_k * sin_one, sin_k * cos_one + cos_k * sin_one

    lax.fori_loop(0, BINS, bin_step, (cos_one, sin_one), unroll=4)

    if last:
        wide = 4
        for step in range(trials // wide):
            block = jnp.concatenate(
                [total_ref[pl.ds(step * wide + j, FRAMES, stride=trials), :] for j in range(wide)], axis=1
            )
            high, low = halves(block)
            series = jnp.dot(
                inverse_ref[...], jnp.concatenate([high, low, high], axis=0), preferred_element_type=jnp.float32
            )
            for j in range(wide):
                out_ref[pl.ds((step * wide + j) * FRAMES, FRAMES), :] = series[:, j * LANES : (j + 1) * LANES]


def dedisperse(spectra, cos_one, sin_one, inverse, held, last):
    each = spectra.shape[1]
    trials, chans = cos_one.shape
    rows = trials * FRAMES
    args = [spectra.reshape(chans * each, LANES), cos_one, sin_one, inverse]
    if held is not None:
        args.append(held)
    scratch = [pltpu.VMEM((FRAMES * chans, LANES), jnp.float32)]
    if last:
        scratch.append(pltpu.VMEM((rows, LANES), jnp.float32))
    return pl.pallas_call(
        functools.partial(
            dedisperse_kernel, chans=chans, each=each, trials=trials, first=held is None, last=last
        ),
        in_specs=[pl.BlockSpec(memory_space=pltpu.VMEM)] * len(args),
        out_specs=pl.BlockSpec(memory_space=pltpu.VMEM),
        out_shape=jax.ShapeDtypeStruct((rows, LANES), jnp.float32),
        scratch_shapes=scratch,
        compiler_params=pltpu.CompilerParams(vmem_limit_bytes=VMEM_LIMIT),
        cost_estimate=pl.CostEstimate(
            flops=BINS * 2 * trials * chans * 2 * LANES * 6, bytes_accessed=spectra.size * 8, transcendentals=0
        ),
        name="dedisperse",
    )(*args)


def sizes_of(total, step):
    if total < 2 * step or total % step or step % 2:
        step = math.gcd(total, max(step // 2, 1))
        return [step] * (total // step)
    return [step // 2] + [step] * (total // step - 1) + [step // 2]


def body(voltages, feed_cells, delays):
    band_chans = voltages.shape[0]
    bands, devices = lax.axis_size("band"), lax.axis_size("feed")
    half = devices // 2
    place = lax.axis_index("feed")
    side = place // half
    spot = place % half
    groups = [list(range(half)), list(range(half, devices))]
    partners = spot ^ jnp.arange(half, dtype=jnp.int32)
    opposite = [(j, (j + half) % devices) for j in range(devices)]
    own_chans = band_chans // half
    cells = lax.dynamic_slice_in_dim(feed_cells[:FEEDS], side * (FEEDS // 2), FEEDS // 2)

    beam_rows = SIDE // 2 // half
    split_rows = beam_rows % 2 == 0
    order = jnp.arange(SIDE // 2, dtype=jnp.int32)
    if split_rows:
        order = order.reshape(half, 2, beam_rows // 2)[partners].swapaxes(0, 1).reshape(-1)
    else:
        order = order.reshape(half, beam_rows)[partners].reshape(-1)
    natural = jnp.arange(SIDE, dtype=jnp.int32) - SIDE // 2
    kept = jnp.concatenate([order + side * (SIDE // 2), order + (1 - side) * (SIDE // 2)]) - SIDE // 2

    forward, inverse = forward_table(), inverse_table()
    trials = delays.shape[1] // bands
    shifts = lax.all_to_all(delays, "band", split_axis=1, concat_axis=0, tiled=True)
    shifts = shifts.reshape(bands, band_chans, trials)

    sizes = sizes_of(own_chans, CHUNK)
    starts = [sum(sizes[:i]) for i in range(len(sizes))]
    spans = [slice(a * half, (a + cc) * half) for a, cc in zip(starts, sizes)]
    count = len(sizes)
    volts, mine, theirs, came, spectra, gathered = ([None] * count for _ in range(6))
    held = None

    def swapped(part, step):
        return lax.ppermute(part, "feed", [(j, j ^ step) for j in range(devices)])

    def send_volts(i, *after):
        piece = voltages[spans[i]]
        if after:
            piece = lax.optimization_barrier((piece,) + after)[0]
        volts[i] = lax.all_to_all(
            piece, "feed", split_axis=0, concat_axis=0, axis_index_groups=groups, tiled=True
        ).reshape(half, sizes[i], voltages.shape[1], LANES)

    def form_partial(i, *after):
        cc = sizes[i]
        channels = (
            lax.axis_index("band") * band_chans
            + starts[i] * half
            + spot * cc
            + jnp.arange(cc, dtype=jnp.int32)
        )
        first = steering_tables(channels, natural)
        second = steering_tables(channels, kept)
        mine[i], theirs[i] = partial_beams(cells, volts[i], first, second, math.gcd(cc, 8), after)
        came[i] = lax.ppermute(theirs[i], "feed", opposite)

    def form_spectra(i, *after):
        own = beam_spectra(mine[i], came[i], forward, half, split_rows, math.gcd(sizes[i], 4), after)
        spectra[i] = jnp.concatenate([own[0]] + [swapped(own[step], step) for step in range(1, half)])
        gathered[i] = lax.all_gather(spectra[i], "band")

    def fold(i, held):
        each = gathered[i].shape[-2]
        shift = shifts[:, spans[i]].reshape(bands, half, -1, trials)[:, partners].reshape(-1, trials).T.astype(jnp.float32) * (2.0 * math.pi / FRAMES)
        return dedisperse(
            gathered[i].reshape(-1, each, LANES), jnp.cos(shift), jnp.sin(shift), inverse, held, i == count - 1
        )

    for i in range(min(2, count)):
        send_volts(i)
    for i in range(count + 3):
        if i < count:
            form_partial(i)
        if i + 2 < count:
            send_volts(i + 2, theirs[i])
        if 0 <= i - 3 < count:
            held = fold(i - 3, held)
        if 0 <= i - 1 < count:
            form_spectra(i - 1, *([theirs[i]] if i < count else []), *([held] if held is not None and i - 3 < count - 1 else []))
    each = gathered[0].shape[-2]
    return held.reshape(trials, FRAMES, LANES)[:, :, : 2 * each].swapaxes(1, 2)


def solution(mesh):
    placed = (P("band", "feed", None), P(), P("band", None))
    return jax.shard_map(
        body, mesh=mesh, in_specs=placed, out_specs=P("band", "feed", None), check_vma=False
    )
```

```python
import functools
import math

import jax
import jax.numpy as jnp
from jax import lax
from jax.experimental import pallas as pl
from jax.experimental.pallas import tpu as pltpu
from jax.sharding import PartitionSpec as P

FEEDS = 2048
CHANNELS = 768
FRAMES = 64
SIDE = 32
BEAMS = 1024
GRID = 64
BINS = FRAMES // 2
LANES = 2 * FRAMES
CHUNK = 8
VMEM_LIMIT = 56 * 1024 * 1024


def high_low(table):
    high = lax.reduce_precision(table, 8, 7)
    return high.astype(jnp.bfloat16), (table - high).astype(jnp.bfloat16)


def halves(values):
    high = values.astype(jnp.bfloat16)
    return high, (values - high.astype(jnp.float32)).astype(jnp.bfloat16)


def steering_tables(channels, offsets):
    lines = jnp.arange(GRID, dtype=jnp.int32)
    residue = jnp.mod(
        offsets[None, :, None] * lines[None, None, :] * (CHANNELS + channels)[:, None, None],
        GRID * CHANNELS,
    )
    phases = residue.astype(jnp.float32) * (2.0 * math.pi / (GRID * CHANNELS))
    high, low = high_low(jnp.concatenate([jnp.cos(phases), jnp.sin(phases)], axis=1))
    return jnp.concatenate([high, high, low], axis=2)


def turned(values):
    swapped = pltpu.roll(values, FRAMES, 1)
    lane = lax.broadcasted_iota(jnp.int32, swapped.shape, 1)
    return jnp.where(lane < FRAMES, swapped, -swapped)


def taken_kernel(*refs):
    refs[-1][...] = refs[0][...]


def taken(whole, start, size, after):
    step = math.gcd(math.gcd(start, size), 8)
    block = (step,) + whole.shape[1:]
    return pl.pallas_call(
        taken_kernel,
        grid=(size // step,),
        in_specs=[pl.BlockSpec(block, lambda i: (start // step + i, 0, 0))]
        + [pl.BlockSpec(memory_space=pl.ANY)] * len(after),
        out_specs=pl.BlockSpec(block, lambda i: (i, 0, 0)),
        out_shape=jax.ShapeDtypeStruct((size,) + whole.shape[1:], whole.dtype),
        compiler_params=pltpu.CompilerParams(vmem_limit_bytes=VMEM_LIMIT),
        cost_estimate=pl.CostEstimate(
            flops=0, bytes_accessed=2 * size * whole.size // whole.shape[0] * 4, transcendentals=0
        ),
        name="taken",
    )(whole, *after)


def partial_kernel(cells_ref, *refs, senders, start, wide):
    volts_ref, first_ref, second_ref = refs[:3]
    mine_ref, theirs_ref, grid_ref, rows_ref = refs[-4:]
    _, kc, feeds_each, _ = volts_ref.shape
    cells = GRID * GRID

    @pl.when(pl.program_id(0) == 0)
    def _():
        grid_ref[...] = jnp.zeros_like(grid_ref)

    for sender in range(senders):

        volts = volts_ref.at[sender].reshape(kc * feeds_each, LANES)

        def place(feed, _, sender=sender, volts=volts):
            cell = cells_ref[sender * feeds_each + feed]
            value = volts[pl.ds(feed, kc, stride=feeds_each), :]
            grid_ref[pl.ds(cell, kc, stride=cells), :] = value
            return 0

        lax.fori_loop(0, feeds_each, place, 0, unroll=8)

    def one_channel(chan, _):
        at_table = start + pl.program_id(0) * kc + chan
        first = first_ref[at_table]
        second = second_ref[at_table]

        def column_step(step, _):
            base = chan * cells + step * (wide * GRID)
            block = jnp.concatenate(
                [grid_ref[pl.ds(base + j * GRID, GRID), :] for j in range(wide)], axis=1
            )
            high, low = halves(block)
            sums = jnp.dot(
                first, jnp.concatenate([high, low, high], axis=0), preferred_element_type=jnp.float32
            )
            for j in range(wide):
                part = sums[:, j * LANES : (j + 1) * LANES]
                rows_ref[pl.ds(step * wide + j, SIDE, stride=GRID), :] = part[:SIDE] + turned(part[SIDE:])
            return 0

        lax.fori_loop(0, GRID // wide, column_step, 0, unroll=True)

        def row_step(step, _):
            base = step * (wide * GRID)
            block = jnp.concatenate(
                [rows_ref[pl.ds(base + j * GRID, GRID), :] for j in range(wide)], axis=1
            )
            high, low = halves(block)
            sums = jnp.dot(
                second, jnp.concatenate([high, low, high], axis=0), preferred_element_type=jnp.float32
            )
            for j in range(wide):
                part = sums[:, j * LANES : (j + 1) * LANES]
                beams = part[:SIDE] + turned(part[SIDE:])
                at = chan * (SIDE // 2 * SIDE) + step * wide + j
                mine_ref[pl.ds(at, SIDE // 2, stride=SIDE), :] = beams[: SIDE // 2]
                theirs_ref[pl.ds(at, SIDE // 2, stride=SIDE), :] = beams[SIDE // 2 :]
            return 0

        lax.fori_loop(0, SIDE // wide, row_step, 0, unroll=True)
        return 0

    lax.fori_loop(0, kc, one_channel, 0)


def partial_beams(cells, volts, first, second, start, after, wide=4):
    senders, cc, feeds_each, _ = volts.shape
    kc = cc if cc <= 8 else math.gcd(cc, 8)
    rows = SIDE // 2 * SIDE
    out = jax.ShapeDtypeStruct((cc * rows, LANES), jnp.float32)
    table_spec = pl.BlockSpec(first.shape, lambda i, *_: (0, 0, 0))
    out_spec = pl.BlockSpec((kc * rows, LANES), lambda i, *_: (i, 0))
    return pl.pallas_call(
        functools.partial(partial_kernel, senders=senders, start=start, wide=wide),
        grid_spec=pltpu.PrefetchScalarGridSpec(
            num_scalar_prefetch=1,
            grid=(cc // kc,),
            in_specs=[
                pl.BlockSpec((senders, kc, feeds_each, LANES), lambda i, *_: (0, i, 0, 0)),
                table_spec,
                table_spec,
            ]
            + [pl.BlockSpec(memory_space=pl.ANY)] * len(after),
            out_specs=[out_spec, out_spec],
            scratch_shapes=[
                pltpu.VMEM((kc * GRID * GRID, LANES), jnp.float32),
                pltpu.VMEM((SIDE * GRID, LANES), jnp.float32),
            ],
        ),
        out_shape=[out, out],
        compiler_params=pltpu.CompilerParams(vmem_limit_bytes=VMEM_LIMIT),
        cost_estimate=pl.CostEstimate(flops=int(cc * 3.9e9 * 10), bytes_accessed=0, transcendentals=0),
        name="partial_beams",
    )(cells, volts, first, second, *after)


def forward_table():
    frames = jnp.arange(FRAMES, dtype=jnp.int32)
    wave = jnp.mod(frames[:, None] * (1 + jnp.arange(BINS, dtype=jnp.int32))[None, :], FRAMES)
    phases = wave.astype(jnp.float32) * (2.0 * math.pi / FRAMES)
    one = jnp.concatenate([jnp.cos(phases), -jnp.sin(phases)], axis=1)
    none = jnp.zeros_like(one)
    both = jnp.concatenate(
        [jnp.concatenate([one, none], axis=1), jnp.concatenate([none, one], axis=1)], axis=0
    )
    high, low = high_low(both)
    return jnp.concatenate([high, high, low], axis=0)


def inverse_table():
    frames = jnp.arange(FRAMES, dtype=jnp.int32)
    bins = 1 + jnp.arange(BINS, dtype=jnp.int32)
    wave = jnp.mod(frames[:, None] * bins[None, :], FRAMES)
    phases = wave.astype(jnp.float32) * (2.0 * math.pi / FRAMES)
    weight = jnp.where(bins < BINS, 2.0, 1.0) * (0.5 / (FRAMES * math.sqrt(CHANNELS) * FEEDS))
    high, low = high_low(jnp.concatenate([jnp.cos(phases) * weight, -jnp.sin(phases) * weight], axis=1))
    return jnp.concatenate([high, high, low], axis=1)


def spectra_kernel(mine_ref, came_ref, table_ref, *refs, kc, split_rows, owners):
    out_refs = refs[-owners:]
    each = out_refs[0].shape[1]
    rows = SIDE // 2 * SIDE
    for chan in range(kc):
        at = pl.ds(chan * rows, rows)
        beams = mine_ref[at, :] + came_ref[at, :]
        square = beams * beams
        power = square + pltpu.roll(square, FRAMES, 1)
        if split_rows:
            left, right = power[: rows // 2], power[rows // 2 :]
        else:
            power = power.reshape(SIDE // 2, 2, SIDE // 2, LANES)
            left = power[:, 0].reshape(rows // 2, LANES)
            right = power[:, 1].reshape(rows // 2, LANES)
        lane = lax.broadcasted_iota(jnp.int32, left.shape, 1)
        high, low = halves(jnp.where(lane < FRAMES, left, right))
        spectra = jnp.dot(
            jnp.concatenate([high, low, high], axis=1), table_ref[...], preferred_element_type=jnp.float32
        )
        for owner in range(owners):
            out_refs[owner][chan] = spectra[owner * each : (owner + 1) * each]


def beam_spectra(mine, came, table, owners, split_rows, kc, after):
    rows = SIDE // 2 * SIDE
    cc = mine.shape[0] // rows
    each = rows // 2 // owners
    block = pl.BlockSpec((kc * rows, LANES), lambda i: (i, 0))
    return pl.pallas_call(
        functools.partial(spectra_kernel, kc=kc, split_rows=split_rows, owners=owners),
        grid=(cc // kc,),
        in_specs=[block, block, pl.BlockSpec(table.shape, lambda i: (0, 0))]
        + [pl.BlockSpec(memory_space=pl.ANY)] * len(after),
        out_specs=[pl.BlockSpec((kc, each, LANES), lambda i: (i, 0, 0))] * owners,
        out_shape=[jax.ShapeDtypeStruct((cc, each, LANES), jnp.float32)] * owners,
        compiler_params=pltpu.CompilerParams(vmem_limit_bytes=VMEM_LIMIT),
        cost_estimate=pl.CostEstimate(flops=int(cc * 5e8 * 10), bytes_accessed=0, transcendentals=0),
        name="beam_spectra",
    )(mine, came, table, *after)


def joined_kernel(slots_ref, *refs, parts):
    rows = refs[0].shape[0]
    for j in range(parts):
        refs[-1][pl.ds(slots_ref[j] * rows, rows)] = refs[j][...]


def joined(slots, parts, after):
    rows = parts[0].shape[0]
    return pl.pallas_call(
        functools.partial(joined_kernel, parts=len(parts)),
        grid_spec=pltpu.PrefetchScalarGridSpec(
            num_scalar_prefetch=1,
            grid=(),
            in_specs=[pl.BlockSpec(memory_space=pltpu.VMEM)] * len(parts)
            + [pl.BlockSpec(memory_space=pl.ANY)] * len(after),
            out_specs=pl.BlockSpec(memory_space=pltpu.VMEM),
        ),
        out_shape=jax.ShapeDtypeStruct((rows * len(parts),) + parts[0].shape[1:], jnp.float32),
        compiler_params=pltpu.CompilerParams(vmem_limit_bytes=VMEM_LIMIT),
        cost_estimate=pl.CostEstimate(flops=int(3e9 * 10), bytes_accessed=0, transcendentals=0),
        name="joined",
    )(slots, *parts, *after)


def dedisperse_kernel(*refs, chans, each, trials, span, first, last):
    spectra_ref, cos_ref, sin_ref, inverse_ref = refs[:4]
    held_ref = None if first else refs[4]
    out_ref, bins_ref = refs[-3 if last else -2], refs[-1 if not last else -2]
    total_ref = refs[-1] if last else out_ref
    stack = LANES // each

    def turn_step(step, _):
        block = jnp.transpose(spectra_ref[pl.ds(step * LANES, LANES), :])
        top, bottom = block[:FRAMES], block[FRAMES:]
        lane = lax.broadcasted_iota(jnp.int32, top.shape, 1)
        for e in range(stack):
            left = pltpu.roll(top, (LANES - e * each) % LANES, 1) if e else top
            shift = (each - e * each) % LANES
            right = pltpu.roll(bottom, shift, 1) if shift else bottom
            bins_ref[pl.ds(step * stack + e, FRAMES, stride=chans), :] = jnp.where(lane < each, left, right)
        return 0

    lax.fori_loop(0, chans // stack, turn_step, 0, unroll=4)

    turns = jnp.concatenate(
        [ref[:, span, :].reshape(chans, trials) for ref in (cos_ref, sin_ref)], axis=1
    )
    turns = jnp.transpose(turns)
    cos_one, sin_one = turns[:trials], turns[trials:]

    def bin_step(k, carry):
        cos_k, sin_k = carry
        shift_high, shift_low = halves(jnp.concatenate([cos_k, sin_k], axis=0))
        spec = jnp.concatenate(
            [bins_ref[pl.ds(k * chans, chans), :], bins_ref[pl.ds((BINS + k) * chans, chans), :]], axis=1
        )
        high, low = halves(spec)
        if chans % LANES == 0:
            sums = jnp.dot(
                jnp.concatenate([shift_high, shift_high, shift_low], axis=1),
                jnp.concatenate([high, low, high], axis=0),
                preferred_element_type=jnp.float32,
            )
        else:
            sums = jnp.dot(shift_high, high, preferred_element_type=jnp.float32)
            sums = sums + jnp.dot(shift_high, low, preferred_element_type=jnp.float32)
            sums = sums + jnp.dot(shift_low, high, preferred_element_type=jnp.float32)
        real = sums[:trials, :LANES] - sums[trials:, LANES:]
        imag = sums[:trials, LANES:] + sums[trials:, :LANES]
        at_real, at_imag = pl.ds(k * trials, trials), pl.ds((BINS + k) * trials, trials)
        if held_ref is not None:
            real = real + held_ref[at_real, :]
            imag = imag + held_ref[at_imag, :]
        total_ref[at_real, :] = real
        total_ref[at_imag, :] = imag
        return cos_k * cos_one - sin_k * sin_one, sin_k * cos_one + cos_k * sin_one

    lax.fori_loop(0, BINS, bin_step, (cos_one, sin_one), unroll=4)

    if last:
        wide = 4
        for step in range(trials // wide):
            block = jnp.concatenate(
                [total_ref[pl.ds(step * wide + j, FRAMES, stride=trials), :] for j in range(wide)], axis=1
            )
            high, low = halves(block)
            series = jnp.dot(
                inverse_ref[...], jnp.concatenate([high, low, high], axis=0), preferred_element_type=jnp.float32
            )
            for j in range(wide):
                out_ref[pl.ds((step * wide + j) * FRAMES, FRAMES), :] = series[:, j * LANES : (j + 1) * LANES]


def dedisperse(spectra, cos_one, sin_one, span, inverse, held, last):
    chans, each, _ = spectra.shape
    trials = cos_one.shape[2]
    rows = trials * FRAMES
    args = [spectra.reshape(chans * each, LANES), cos_one, sin_one, inverse]
    if held is not None:
        args.append(held)
    scratch = [pltpu.VMEM((FRAMES * chans, LANES), jnp.float32)]
    if last:
        scratch.append(pltpu.VMEM((rows, LANES), jnp.float32))
    return pl.pallas_call(
        functools.partial(
            dedisperse_kernel, chans=chans, each=each, trials=trials, span=span, first=held is None, last=last
        ),
        in_specs=[pl.BlockSpec(memory_space=pltpu.VMEM)] * len(args),
        out_specs=pl.BlockSpec(memory_space=pltpu.VMEM),
        out_shape=jax.ShapeDtypeStruct((rows, LANES), jnp.float32),
        scratch_shapes=scratch,
        compiler_params=pltpu.CompilerParams(vmem_limit_bytes=VMEM_LIMIT),
        cost_estimate=pl.CostEstimate(flops=int(1.3e10 * 10), bytes_accessed=0, transcendentals=0),
        name="dedisperse",
    )(*args)


def sizes_of(total, step):
    if total < 2 * step or total % step or step % 2:
        step = math.gcd(total, max(step // 2, 1))
        return [step] * (total // step)
    return [step // 2] + [step] * (total // step - 1) + [step // 2]


def body(voltages, feed_cells, delays):
    band_chans = voltages.shape[0]
    bands, devices = lax.axis_size("band"), lax.axis_size("feed")
    half = devices // 2
    place = lax.axis_index("feed")
    side = place // half
    spot = place % half
    groups = [list(range(half)), list(range(half, devices))]
    partners = spot ^ jnp.arange(half, dtype=jnp.int32)
    opposite = [(j, (j + half) % devices) for j in range(devices)]
    own_chans = band_chans // half
    cells = lax.dynamic_slice_in_dim(feed_cells[:FEEDS], side * (FEEDS // 2), FEEDS // 2)

    beam_rows = SIDE // 2 // half
    split_rows = beam_rows % 2 == 0
    order = jnp.arange(SIDE // 2, dtype=jnp.int32)
    if split_rows:
        order = order.reshape(half, 2, beam_rows // 2)[partners].swapaxes(0, 1).reshape(-1)
    else:
        order = order.reshape(half, beam_rows)[partners].reshape(-1)
    natural = jnp.arange(SIDE, dtype=jnp.int32) - SIDE // 2
    kept = jnp.concatenate([order + side * (SIDE // 2), order + (1 - side) * (SIDE // 2)]) - SIDE // 2

    forward, inverse = forward_table(), inverse_table()
    trials = delays.shape[1] // bands

    sizes = sizes_of(own_chans, CHUNK)
    starts = [sum(sizes[:i]) for i in range(len(sizes))]
    spans = [slice(a * half, (a + cc) * half) for a, cc in zip(starts, sizes)]
    count = len(sizes)
    volts, mine, theirs, came, spectra, gathered = ([None] * count for _ in range(6))
    held = None

    def swapped(part, step):
        return lax.ppermute(part, "feed", [(j, j ^ step) for j in range(devices)])

    channels = jnp.concatenate(
        [a * half + spot * cc + jnp.arange(cc, dtype=jnp.int32) for a, cc in zip(starts, sizes)]
    ) + lax.axis_index("band") * band_chans
    first = steering_tables(channels, natural)
    second = steering_tables(channels, kept)

    def send_volts(i, *after):
        piece = taken(voltages, starts[i] * half, sizes[i] * half, after)
        volts[i] = lax.all_to_all(
            piece, "feed", split_axis=0, concat_axis=0, axis_index_groups=groups, tiled=True
        ).reshape(half, sizes[i], voltages.shape[1], LANES)

    def form_partial(i, *after):
        mine[i], theirs[i] = partial_beams(cells, volts[i], first, second, starts[i], after)
        came[i] = lax.ppermute(theirs[i], "feed", opposite)

    def form_spectra(i, *after):
        own = beam_spectra(mine[i], came[i], forward, half, split_rows, math.gcd(sizes[i], 4), after)
        spectra[i] = [own[0]] + [swapped(own[step], step) for step in range(1, half)]

    def gather_spectra(i, *after):
        gathered[i] = lax.all_gather(joined(partners, spectra[i], after), "band")

    def fold(i, held):
        each = gathered[i].shape[-2]
        return dedisperse(
            gathered[i].reshape(-1, each, LANES), shift_cos, shift_sin, spans[i], inverse, held, i == count - 1
        )

    for i in range(min(2, count)):
        send_volts(i)
    for i in range(count + 3):
        if i < count:
            form_partial(i)
        if i == 0:
            shifts = lax.all_gather(delays, "band")
            shifts = lax.dynamic_slice_in_dim(shifts, lax.axis_index("band") * trials, trials, 2)
            shifts = shifts.astype(jnp.float32) * (2.0 * math.pi / FRAMES)
            shift_cos, shift_sin = jnp.cos(shifts), jnp.sin(shifts)
        if i + 2 < count:
            send_volts(i + 2, theirs[i])
        if 0 <= i - 2 < count:
            gather_spectra(i - 2, *([theirs[i]] if i < count else []))
        if 0 <= i - 3 < count:
            held = fold(i - 3, held)
        if 0 <= i - 1 < count:
            form_spectra(i - 1, *([theirs[i]] if i < count else []), *([held] if held is not None else []))
    each = gathered[0].shape[-2]
    return held.reshape(trials, FRAMES, LANES)[:, :, : 2 * each].swapaxes(1, 2)


def solution(mesh):
    placed = (P("band", "feed", None), P(), P("band", None))
    return jax.shard_map(
        body, mesh=mesh, in_specs=placed, out_specs=P("band", "feed", None), check_vma=False
    )
```

```python
import functools
import math

import jax
import jax.numpy as jnp
from jax import lax
from jax.experimental import pallas as pl
from jax.experimental.pallas import tpu as pltpu
from jax.sharding import PartitionSpec as P

FEEDS = 2048
CHANNELS = 768
FRAMES = 64
SIDE = 32
BEAMS = 1024
GRID = 64
BINS = FRAMES // 2
LANES = 2 * FRAMES
VMEM_LIMIT = 56 * 1024 * 1024


def high_low(table):
    high = lax.reduce_precision(table, 8, 7)
    return high.astype(jnp.bfloat16), (table - high).astype(jnp.bfloat16)


def halves(values):
    high = values.astype(jnp.bfloat16)
    return high, (values - high.astype(jnp.float32)).astype(jnp.bfloat16)


def steering_tables(channels, offsets):
    lines = jnp.arange(GRID, dtype=jnp.int32)
    residue = jnp.mod(
        offsets[None, :, None] * lines[None, None, :] * (CHANNELS + channels)[:, None, None],
        GRID * CHANNELS,
    )
    phases = residue.astype(jnp.float32) * (2.0 * math.pi / (GRID * CHANNELS))
    high, low = high_low(jnp.concatenate([jnp.cos(phases), jnp.sin(phases)], axis=1))
    return jnp.concatenate([high, high, low], axis=2)


def turned(values):
    swapped = pltpu.roll(values, FRAMES, 1)
    lane = lax.broadcasted_iota(jnp.int32, swapped.shape, 1)
    return jnp.where(lane < FRAMES, swapped, -swapped)


def taken_kernel(*refs):
    refs[-1][...] = refs[0][...]


def taken(whole, start, size, after):
    step = math.gcd(math.gcd(start, size), 8)
    block = (step,) + whole.shape[1:]
    return pl.pallas_call(
        taken_kernel,
        grid=(size // step,),
        in_specs=[pl.BlockSpec(block, lambda i: (start // step + i, 0, 0))]
        + [pl.BlockSpec(memory_space=pl.ANY)] * len(after),
        out_specs=pl.BlockSpec(block, lambda i: (i, 0, 0)),
        out_shape=jax.ShapeDtypeStruct((size,) + whole.shape[1:], whole.dtype),
        compiler_params=pltpu.CompilerParams(vmem_limit_bytes=VMEM_LIMIT),
        cost_estimate=pl.CostEstimate(
            flops=0, bytes_accessed=2 * size * whole.size // whole.shape[0] * 4, transcendentals=0
        ),
        name="taken",
    )(whole, *after)


def partial_kernel(cells_ref, *refs, senders, start, wide):
    volts_ref, first_ref, second_ref = refs[:3]
    mine_ref, theirs_ref, grid_ref, rows_ref = refs[-4:]
    _, kc, feeds_each, _ = volts_ref.shape
    cells = GRID * GRID

    @pl.when(pl.program_id(0) == 0)
    def _():
        grid_ref[...] = jnp.zeros_like(grid_ref)

    for sender in range(senders):

        volts = volts_ref.at[sender].reshape(kc * feeds_each, LANES)

        def place(feed, _, sender=sender, volts=volts):
            cell = cells_ref[sender * feeds_each + feed]
            value = volts[pl.ds(feed, kc, stride=feeds_each), :]
            grid_ref[pl.ds(cell, kc, stride=cells), :] = value
            return 0

        lax.fori_loop(0, feeds_each, place, 0, unroll=8)

    def one_channel(chan, _):
        at_table = start + pl.program_id(0) * kc + chan
        first = first_ref[at_table]
        second = second_ref[at_table]

        def column_step(step, _):
            base = chan * cells + step * (wide * GRID)
            block = jnp.concatenate(
                [grid_ref[pl.ds(base + j * GRID, GRID), :] for j in range(wide)], axis=1
            )
            high, low = halves(block)
            sums = jnp.dot(
                first, jnp.concatenate([high, low, high], axis=0), preferred_element_type=jnp.float32
            )
            for j in range(wide):
                part = sums[:, j * LANES : (j + 1) * LANES]
                rows_ref[pl.ds(step * wide + j, SIDE, stride=GRID), :] = part[:SIDE] + turned(part[SIDE:])
            return 0

        lax.fori_loop(0, GRID // wide, column_step, 0, unroll=True)

        def row_step(step, _):
            base = step * (wide * GRID)
            block = jnp.concatenate(
                [rows_ref[pl.ds(base + j * GRID, GRID), :] for j in range(wide)], axis=1
            )
            high, low = halves(block)
            sums = jnp.dot(
                second, jnp.concatenate([high, low, high], axis=0), preferred_element_type=jnp.float32
            )
            for j in range(wide):
                part = sums[:, j * LANES : (j + 1) * LANES]
                beams = part[:SIDE] + turned(part[SIDE:])
                at = chan * (SIDE // 2 * SIDE) + step * wide + j
                mine_ref[pl.ds(at, SIDE // 2, stride=SIDE), :] = beams[: SIDE // 2]
                theirs_ref[pl.ds(at, SIDE // 2, stride=SIDE), :] = beams[SIDE // 2 :]
            return 0

        lax.fori_loop(0, SIDE // wide, row_step, 0, unroll=True)
        return 0

    lax.fori_loop(0, kc, one_channel, 0)


def partial_beams(cells, volts, first, second, start, after, wide=4):
    senders, cc, feeds_each, _ = volts.shape
    kc = cc if cc <= 8 else math.gcd(cc, 8)
    rows = SIDE // 2 * SIDE
    out = jax.ShapeDtypeStruct((cc * rows, LANES), jnp.float32)
    table_spec = pl.BlockSpec(first.shape, lambda i, *_: (0, 0, 0))
    out_spec = pl.BlockSpec((kc * rows, LANES), lambda i, *_: (i, 0))
    return pl.pallas_call(
        functools.partial(partial_kernel, senders=senders, start=start, wide=wide),
        grid_spec=pltpu.PrefetchScalarGridSpec(
            num_scalar_prefetch=1,
            grid=(cc // kc,),
            in_specs=[
                pl.BlockSpec((senders, kc, feeds_each, LANES), lambda i, *_: (0, i, 0, 0)),
                table_spec,
                table_spec,
            ]
            + [pl.BlockSpec(memory_space=pl.ANY)] * len(after),
            out_specs=[out_spec, out_spec],
            scratch_shapes=[
                pltpu.VMEM((kc * GRID * GRID, LANES), jnp.float32),
                pltpu.VMEM((SIDE * GRID, LANES), jnp.float32),
            ],
        ),
        out_shape=[out, out],
        compiler_params=pltpu.CompilerParams(vmem_limit_bytes=VMEM_LIMIT),
        cost_estimate=pl.CostEstimate(flops=int(cc * 3.9e10), bytes_accessed=0, transcendentals=0),
        name="partial_beams",
    )(cells, volts, first, second, *after)


def forward_table():
    frames = jnp.arange(FRAMES, dtype=jnp.int32)
    wave = jnp.mod(frames[:, None] * (1 + jnp.arange(BINS, dtype=jnp.int32))[None, :], FRAMES)
    phases = wave.astype(jnp.float32) * (2.0 * math.pi / FRAMES)
    one = jnp.concatenate([jnp.cos(phases), -jnp.sin(phases)], axis=1)
    none = jnp.zeros_like(one)
    both = jnp.concatenate(
        [jnp.concatenate([one, none], axis=1), jnp.concatenate([none, one], axis=1)], axis=0
    )
    high, low = high_low(both)
    return jnp.concatenate([high, high, low], axis=0)


def inverse_table():
    frames = jnp.arange(FRAMES, dtype=jnp.int32)
    bins = 1 + jnp.arange(BINS, dtype=jnp.int32)
    wave = jnp.mod(frames[:, None] * bins[None, :], FRAMES)
    phases = wave.astype(jnp.float32) * (2.0 * math.pi / FRAMES)
    weight = jnp.where(bins < BINS, 2.0, 1.0) * (0.5 / (FRAMES * math.sqrt(CHANNELS) * FEEDS))
    high, low = high_low(jnp.concatenate([jnp.cos(phases) * weight, -jnp.sin(phases) * weight], axis=1))
    return jnp.concatenate([high, high, low], axis=1)


def spectra_kernel(mine_ref, came_ref, table_ref, *refs, kc, split_rows, owners):
    out_refs = refs[-owners:]
    each = out_refs[0].shape[1]
    rows = SIDE // 2 * SIDE
    for chan in range(kc):
        at = pl.ds(chan * rows, rows)
        beams = mine_ref[at, :] + came_ref[at, :]
        square = beams * beams
        power = square + pltpu.roll(square, FRAMES, 1)
        if split_rows:
            left, right = power[: rows // 2], power[rows // 2 :]
        else:
            power = power.reshape(SIDE // 2, 2, SIDE // 2, LANES)
            left = power[:, 0].reshape(rows // 2, LANES)
            right = power[:, 1].reshape(rows // 2, LANES)
        lane = lax.broadcasted_iota(jnp.int32, left.shape, 1)
        high, low = halves(jnp.where(lane < FRAMES, left, right))
        spectra = jnp.dot(
            jnp.concatenate([high, low, high], axis=1), table_ref[...], preferred_element_type=jnp.float32
        )
        for owner in range(owners):
            out_refs[owner][chan] = spectra[owner * each : (owner + 1) * each]


def beam_spectra(mine, came, table, owners, split_rows, kc, after):
    rows = SIDE // 2 * SIDE
    cc = mine.shape[0] // rows
    each = rows // 2 // owners
    block = pl.BlockSpec((kc * rows, LANES), lambda i: (i, 0))
    return pl.pallas_call(
        functools.partial(spectra_kernel, kc=kc, split_rows=split_rows, owners=owners),
        grid=(cc // kc,),
        in_specs=[block, block, pl.BlockSpec(table.shape, lambda i: (0, 0))]
        + [pl.BlockSpec(memory_space=pl.ANY)] * len(after),
        out_specs=[pl.BlockSpec((kc, each, LANES), lambda i: (i, 0, 0))] * owners,
        out_shape=[jax.ShapeDtypeStruct((cc, each, LANES), jnp.float32)] * owners,
        compiler_params=pltpu.CompilerParams(vmem_limit_bytes=VMEM_LIMIT),
        cost_estimate=pl.CostEstimate(flops=int(cc * 5e9), bytes_accessed=0, transcendentals=0),
        name="beam_spectra",
    )(mine, came, table, *after)


def joined_kernel(slots_ref, *refs, parts):
    rows = refs[0].shape[0]
    for j in range(parts):
        refs[-1][pl.ds(slots_ref[j] * rows, rows)] = refs[j][...]


def joined(slots, parts, after):
    rows = parts[0].shape[0]
    return pl.pallas_call(
        functools.partial(joined_kernel, parts=len(parts)),
        grid_spec=pltpu.PrefetchScalarGridSpec(
            num_scalar_prefetch=1,
            grid=(),
            in_specs=[pl.BlockSpec(memory_space=pltpu.VMEM)] * len(parts)
            + [pl.BlockSpec(memory_space=pl.ANY)] * len(after),
            out_specs=pl.BlockSpec(memory_space=pltpu.VMEM),
        ),
        out_shape=jax.ShapeDtypeStruct((rows * len(parts),) + parts[0].shape[1:], jnp.float32),
        compiler_params=pltpu.CompilerParams(vmem_limit_bytes=VMEM_LIMIT),
        cost_estimate=pl.CostEstimate(flops=int(3e10), bytes_accessed=0, transcendentals=0),
        name="joined",
    )(slots, *parts, *after)


def dedisperse_kernel(*refs, chans, each, trials, span, first, last):
    spectra_ref, cos_ref, sin_ref, inverse_ref = refs[:4]
    held_ref = None if first else refs[4]
    out_ref, bins_ref = refs[-3 if last else -2], refs[-1 if not last else -2]
    total_ref = refs[-1] if last else out_ref
    stack = LANES // each

    def turn_step(step, _):
        block = jnp.transpose(spectra_ref[pl.ds(step * LANES, LANES), :])
        top, bottom = block[:FRAMES], block[FRAMES:]
        lane = lax.broadcasted_iota(jnp.int32, top.shape, 1)
        for e in range(stack):
            left = pltpu.roll(top, (LANES - e * each) % LANES, 1) if e else top
            shift = (each - e * each) % LANES
            right = pltpu.roll(bottom, shift, 1) if shift else bottom
            bins_ref[pl.ds(step * stack + e, FRAMES, stride=chans), :] = jnp.where(lane < each, left, right)
        return 0

    lax.fori_loop(0, chans // stack, turn_step, 0, unroll=min(16, chans // stack) if last else 4)

    turns = jnp.concatenate(
        [ref[:, span, :].reshape(chans, trials) for ref in (cos_ref, sin_ref)], axis=1
    )
    turns = jnp.transpose(turns)
    cos_one, sin_one = turns[:trials], turns[trials:]

    def bin_step(k, carry):
        cos_k, sin_k = carry
        shift_high, shift_low = halves(jnp.concatenate([cos_k, sin_k], axis=0))
        spec = jnp.concatenate(
            [bins_ref[pl.ds(k * chans, chans), :], bins_ref[pl.ds((BINS + k) * chans, chans), :]], axis=1
        )
        high, low = halves(spec)
        if chans % LANES == 0:
            sums = jnp.dot(
                jnp.concatenate([shift_high, shift_high, shift_low], axis=1),
                jnp.concatenate([high, low, high], axis=0),
                preferred_element_type=jnp.float32,
            )
        else:
            sums = jnp.dot(shift_high, high, preferred_element_type=jnp.float32)
            sums = sums + jnp.dot(shift_high, low, preferred_element_type=jnp.float32)
            sums = sums + jnp.dot(shift_low, high, preferred_element_type=jnp.float32)
        real = sums[:trials, :LANES] - sums[trials:, LANES:]
        imag = sums[:trials, LANES:] + sums[trials:, :LANES]
        at_real, at_imag = pl.ds(k * trials, trials), pl.ds((BINS + k) * trials, trials)
        if held_ref is not None:
            real = real + held_ref[at_real, :]
            imag = imag + held_ref[at_imag, :]
        total_ref[at_real, :] = real
        total_ref[at_imag, :] = imag
        return cos_k * cos_one - sin_k * sin_one, sin_k * cos_one + cos_k * sin_one

    lax.fori_loop(0, BINS, bin_step, (cos_one, sin_one), unroll=True if last else 4)

    if last:
        wide = 4
        for step in range(trials // wide):
            block = jnp.concatenate(
                [total_ref[pl.ds(step * wide + j, FRAMES, stride=trials), :] for j in range(wide)], axis=1
            )
            high, low = halves(block)
            series = jnp.dot(
                inverse_ref[...], jnp.concatenate([high, low, high], axis=0), preferred_element_type=jnp.float32
            )
            for j in range(wide):
                out_ref[pl.ds((step * wide + j) * FRAMES, FRAMES), :] = series[:, j * LANES : (j + 1) * LANES]


def dedisperse(spectra, cos_one, sin_one, span, inverse, held, last):
    chans, each, _ = spectra.shape
    trials = cos_one.shape[2]
    rows = trials * FRAMES
    args = [spectra.reshape(chans * each, LANES), cos_one, sin_one, inverse]
    if held is not None:
        args.append(held)
    scratch = [pltpu.VMEM((FRAMES * chans, LANES), jnp.float32)]
    if last:
        scratch.append(pltpu.VMEM((rows, LANES), jnp.float32))
    return pl.pallas_call(
        functools.partial(
            dedisperse_kernel, chans=chans, each=each, trials=trials, span=span, first=held is None, last=last
        ),
        in_specs=[pl.BlockSpec(memory_space=pltpu.VMEM)] * len(args),
        out_specs=pl.BlockSpec(memory_space=pltpu.VMEM),
        out_shape=jax.ShapeDtypeStruct((rows, LANES), jnp.float32),
        scratch_shapes=scratch,
        compiler_params=pltpu.CompilerParams(vmem_limit_bytes=VMEM_LIMIT),
        cost_estimate=pl.CostEstimate(flops=int(1.3e11), bytes_accessed=0, transcendentals=0),
        name="dedisperse",
    )(*args)


def sizes_of(total, half):
    shares = (2, 4, 4, 4, 4, 3, 2, 1)
    unit, rest = divmod(total, sum(shares))
    if unit and not rest and unit * half % 8 == 0:
        return [unit * share for share in shares]
    step = math.gcd(total, 4)
    return [step] * (total // step)


def body(voltages, feed_cells, delays):
    band_chans = voltages.shape[0]
    bands, devices = lax.axis_size("band"), lax.axis_size("feed")
    half = devices // 2
    place = lax.axis_index("feed")
    side = place // half
    spot = place % half
    groups = [list(range(half)), list(range(half, devices))]
    partners = spot ^ jnp.arange(half, dtype=jnp.int32)
    opposite = [(j, (j + half) % devices) for j in range(devices)]
    own_chans = band_chans // half
    cells = lax.dynamic_slice_in_dim(feed_cells[:FEEDS], side * (FEEDS // 2), FEEDS // 2)

    beam_rows = SIDE // 2 // half
    split_rows = beam_rows % 2 == 0
    order = jnp.arange(SIDE // 2, dtype=jnp.int32)
    if split_rows:
        order = order.reshape(half, 2, beam_rows // 2)[partners].swapaxes(0, 1).reshape(-1)
    else:
        order = order.reshape(half, beam_rows)[partners].reshape(-1)
    natural = jnp.arange(SIDE, dtype=jnp.int32) - SIDE // 2
    kept = jnp.concatenate([order + side * (SIDE // 2), order + (1 - side) * (SIDE // 2)]) - SIDE // 2

    forward, inverse = forward_table(), inverse_table()
    trials = delays.shape[1] // bands

    sizes = sizes_of(own_chans, half)
    starts = [sum(sizes[:i]) for i in range(len(sizes))]
    spans = [slice(a * half, (a + cc) * half) for a, cc in zip(starts, sizes)]
    count = len(sizes)
    volts, mine, theirs, came, spectra, gathered = ([None] * count for _ in range(6))
    held = None

    def swapped(part, step):
        return lax.ppermute(part, "feed", [(j, j ^ step) for j in range(devices)])

    channels = jnp.concatenate(
        [a * half + spot * cc + jnp.arange(cc, dtype=jnp.int32) for a, cc in zip(starts, sizes)]
    ) + lax.axis_index("band") * band_chans
    first = steering_tables(channels, natural)
    second = steering_tables(channels, kept)

    def send_volts(i, *after):
        piece = taken(voltages, starts[i] * half, sizes[i] * half, after)
        volts[i] = lax.all_to_all(
            piece, "feed", split_axis=0, concat_axis=0, axis_index_groups=groups, tiled=True
        ).reshape(half, sizes[i], voltages.shape[1], LANES)

    def form_partial(i, *after):
        mine[i], theirs[i] = partial_beams(cells, volts[i], first, second, starts[i], after)
        came[i] = lax.ppermute(theirs[i], "feed", opposite)

    def form_spectra(i, *after):
        own = beam_spectra(mine[i], came[i], forward, half, split_rows, math.gcd(sizes[i], 4), after)
        spectra[i] = [own[0]] + [swapped(own[step], step) for step in range(1, half)]

    def gather_spectra(i, *after):
        gathered[i] = lax.all_gather(joined(partners, spectra[i], after), "band")

    def fold(i, held):
        each = gathered[i].shape[-2]
        return dedisperse(
            gathered[i].reshape(-1, each, LANES), shift_cos, shift_sin, spans[i], inverse, held, i == count - 1
        )

    for i in range(min(2, count)):
        send_volts(i)
    for i in range(count + 3):
        if i < count:
            form_partial(i)
        if i == 0:
            shifts = lax.all_gather(delays, "band")
            shifts = lax.dynamic_slice_in_dim(shifts, lax.axis_index("band") * trials, trials, 2)
            shifts = shifts.astype(jnp.float32) * (2.0 * math.pi / FRAMES)
            shift_cos, shift_sin = jnp.cos(shifts), jnp.sin(shifts)
        if i + 2 < count:
            send_volts(i + 2, theirs[i])
        if 0 <= i - 2 < count:
            gather_spectra(i - 2, *([theirs[i]] if i < count else []))
        if 0 <= i - 3 < count:
            held = fold(i - 3, held)
        if 0 <= i - 1 < count:
            form_spectra(i - 1, *([theirs[i]] if i < count else []), *([held] if held is not None else []))
    each = gathered[0].shape[-2]
    return held.reshape(trials, FRAMES, LANES)[:, :, : 2 * each].swapaxes(1, 2)


def solution(mesh):
    placed = (P("band", "feed", None), P(), P("band", None))
    return jax.shard_map(
        body, mesh=mesh, in_specs=placed, out_specs=P("band", "feed", None), check_vma=False
    )
```
